32 devices in a mesh: attn: 4 (over z), expert: 4 (over y, x), rep: 2 (over core).
Axes of the slice: x: 2, y: 2, z: 4, core: 2. Of those that a mesh axis runs over, the one named last changes fastest.
Arguments:
- queries: bfloat16 [32, 73728], P('attn', ('expert', 'rep')), may hold values from -120 to 120
- new_latent: bfloat16 [32, 576], P('attn'), may hold values from -6 to 6
- cache_pool: bfloat16 [2048, 576], P('attn'), may hold values from -6 to 6
- local_len: int32 [4, 4], P('attn'), may hold values from 1 to 384, 512 in all within a row
- spill_cache: bfloat16 [16, 16, 576], P('attn'), may hold values from -6 to 6
- spill_owner: int32 [16], replicated, may hold values from -1 to 15, as said below
- w_uv: bfloat16 [128, 512, 128], P(('expert', 'rep')), may hold values from -0.25 to 0.25
- w_o: bfloat16 [16384, 7168], P(('expert', 'rep'), 'attn'), may hold values from -0.046875 to 0.046875
- residual: bfloat16 [32, 7168], P(None, 'attn'), may hold values from -3 to 3
- norm_gain: float32 [7168], replicated, may hold values from 0.5 to 1.5
- route_ids: int32 [32, 4], replicated, may hold values from 0 to 15, all different within a row; in each aligned block of 16 rows (0 to 15, 16 to 31, ...) at most 5 rows name the same one
- route_scores: float32 [32, 4], replicated, may hold values from 0.05 to 1
- w_gate: bfloat16 [7168, 32768], P(None, ('attn', 'expert')), may hold values from -0.0625 to 0.0625
- w_up: bfloat16 [7168, 32768], P(None, ('attn', 'expert')), may hold values from -0.0625 to 0.0625
- w_down: bfloat16 [32768, 7168], P(('attn', 'expert')), may hold values from -0.125 to 0.125
Outputs:
- mixed: bfloat16 [32, 7168], P('rep', ('attn', 'expert'))
The draws below stay inside these ranges and needn't reach their ends.
Inputs may be any that keep to these rules, and one draw needn't show every extreme that they name: Each row of local_len sums to 512. `spill_owner`: each entry is -1 or the number of a request that lives on another index of attn than the block's slot. The slots of one index of attn hold at most 2 blocks of the requests of any one other index, and some index holds exactly 2 for some other index in every draw. `route_ids`: the token rows fall into 2 aligned blocks of 16 rows in order (2 being the size of rep); in each block no expert is named by more than 5 rows, and in some block one is named by exactly 5.
All inputs are finite; a program needn't handle non-finite values.
Results may differ from the reference program's by a relative error of at most 0.025.
Values may be sent and summed in bfloat16 or wider, within the bound.
A program may use at most 192 MiB of HBM per device.

```python
import math
import jax
import jax.numpy as jnp
import numpy as np
from jax import lax

D = 7168
H = 128
LAT = 512
ROPE = 64
VH = 128
FFE = 2048
EXPERTS = 16
TOP = 4
REQ_DEV = 4
POOL = 512
MAXLOC = 384
BLK = 16
CAP = 2
GROUPS = 2
SPILL = 4
TOKENS = 32
CAPJ = 5
N_ATTN = 4
N_REP = 2


def latent_pair(key):
    base_key = jax.random.fold_in(key, 31)
    key_query, key_latent = jax.random.split(base_key, 2)
    row_width = LAT + ROPE
    query_rows = jax.random.truncated_normal(key_query, -6.0, 6.0, (TOKENS, H, row_width), jnp.float32)
    latent = jax.random.truncated_normal(key_latent, -6.0, 6.0, (TOKENS, row_width), jnp.float32)
    return (query_rows.reshape(TOKENS, H * row_width), latent)


def draw_queries(key, part):
    return latent_pair(key)[0].astype(jnp.bfloat16)


def draw_new_latent(key, part):
    return latent_pair(key)[1].astype(jnp.bfloat16)


def draw_spill_owner(key, part):
    base_key = jax.random.fold_in(key, 53)
    key_perm, key_req, key_keep = jax.random.split(base_key, 3)
    permuted = jax.vmap(lambda sub_key: jax.random.permutation(sub_key, N_ATTN - 1))(jax.random.split(key_perm, N_ATTN))
    first_row = permuted[0]
    rolled = (first_row + (N_ATTN - 2) - first_row[0]) % (N_ATTN - 1)
    permuted = permuted.at[0].set(rolled.astype(permuted.dtype))
    offsets = 1 + permuted[:, :GROUPS]
    host_ids = jnp.arange(N_ATTN, dtype=jnp.int32)[:, None]
    owner_dev = (host_ids + offsets) % N_ATTN
    local_req = jax.random.randint(key_req, (N_ATTN, GROUPS, CAP), 0, REQ_DEV)
    local_req = local_req.at[0, 0, 0].set(REQ_DEV - 1)
    kept = jax.random.randint(key_keep, (N_ATTN, GROUPS, CAP), 0, 4) > 0
    forced = (jnp.arange(CAP) == 0)[None, None, :] | (jnp.arange(GROUPS) == 0)[None, :, None]
    kept = kept | forced
    kept = kept.at[0, GROUPS - 1, CAP - 1].set(False)
    owner_ids = jnp.where(kept, owner_dev[:, :, None] * REQ_DEV + local_req, -1)
    return owner_ids.reshape(N_ATTN * GROUPS * CAP).astype(jnp.int32)


def levels(own_key, shape, cuts, least, top_value):
    def one(dim, blocks):
        heights = jax.random.uniform(jax.random.fold_in(jax.random.fold_in(own_key, 6), dim), (blocks,), jnp.float32, least / len(cuts), top_value / len(cuts))
        return jnp.repeat(jnp.exp(heights), shape[dim] // blocks).reshape((-1,) + (1,) * (len(shape) - dim - 1))

    loudness = one(*cuts[0])
    for cut in cuts[1:]:
        loudness = loudness * one(*cut)
    return loudness


def split_up(count, total, reach, lean):
    loads = [(1 << 20) // math.isqrt(grade ** lean) + 1 for grade in range(2, count + 1)]
    spare, given = total - reach - (count - 1), [1] * (count - 1)
    while spare > 0:
        free = [i for i in range(count - 1) if given[i] < reach]
        whole, left = sum([loads[i] for i in free]), spare
        for i in free:
            extra = min(reach - given[i], max(1, left * loads[i] // whole), spare)
            given[i] = given[i] + extra
            spare = spare - extra
    return np.array([reach] + given)


def ragged(own_key, number_of, total, most, slope):
    if number_of == 2:
        one = jax.random.randint(own_key, (), max(1, total - most), min(most, total - 1) + 1)
        return jnp.stack([one, total - one])
    lengths = jnp.asarray(split_up(number_of, total, most, slope), jnp.int32)
    couples = (number_of - 1) // 2
    donor, taker = lengths[1:1 + 2 * couples:2], lengths[2:2 + 2 * couples:2]
    margin = jnp.minimum(donor - 1, most - taker)
    moved = jax.random.randint(jax.random.fold_in(own_key, 1), (couples,), 0, 1 << 20) % (margin + 1)
    lengths = lengths.at[1:1 + 2 * couples:2].set(donor - moved).at[2:2 + 2 * couples:2].set(taker + moved)
    return lengths[jax.random.permutation(jax.random.fold_in(own_key, 2), number_of)]


def routed_block(stream_key, own, number, rows, count, top, most, skew):
    order = jax.random.permutation(stream_key, count)
    heavy_load, ordinary = portions_of(count, rows * top, most, skew, True), portions_of(count, rows * top, most, skew, False)
    places = jnp.arange(count)

    def named(sizes, rotation):
        used = int((sizes > 0).sum())
        fixed = max(1, used // 4)
        moved = fixed + (places - fixed + rotation * (used - fixed)) % max(1, count - fixed)
        return jnp.zeros((count,), jnp.int32).at[order[jnp.where(places < fixed, places, moved)]].set(jnp.asarray(sizes, jnp.int32))

    sizes = jnp.where(number % 4 == 0, named(heavy_load, number // 4), named(ordinary, number - number // 4 - 1))
    mixed = jax.random.permutation(jax.random.fold_in(own, 3), count)
    giver, taker = mixed[0:count // 2 * 2:2], mixed[1:count // 2 * 2:2]
    slack = jnp.minimum(sizes[giver] - 1, most - sizes[taker]) // 2
    slack = jnp.where((giver == order[0]) | (taker == order[0]) | (sizes[taker] == 0), 0, jnp.maximum(slack, 0))
    moved = jax.random.randint(jax.random.fold_in(own, 4), (count // 2,), 0, 1 << 20) % (slack + 1)
    sizes = sizes.at[giver].add(-moved).at[taker].add(moved)
    labels = jnp.searchsorted(jnp.cumsum(sizes), jnp.arange(rows * top), side="right").astype(jnp.int32)
    table = labels.reshape(top, rows).T
    table = table[jax.random.permutation(jax.random.fold_in(own, 1), rows)]
    rotation = jax.random.randint(jax.random.fold_in(own, 2), (rows, 1), 0, top)
    return jnp.take_along_axis(table, (jnp.arange(top)[None, :] + rotation) % top, axis=1)


def portions_of(count, total, limit, slope, full):
    loads = [(1 << 20) // math.isqrt(rank ** slope) + 1 for rank in range(1, count + 1)]
    largest = limit if full else min(limit, max(-(-total // count), total * loads[0] // sum(loads)))
    least = 1 if total - largest >= count - 1 else 0
    counts, rest = [largest] + [least] * (count - 1), total - largest - least * (count - 1)
    while rest > 0:
        movable = [i for i in range(1, count) if counts[i] < largest] or [i for i in range(1, count) if counts[i] < limit]
        whole, budget = sum([loads[i] for i in movable]), rest
        for i in movable:
            more = min(limit - counts[i], max(1, budget * loads[i] // whole), rest)
            counts[i] = counts[i] + more
            rest = rest - more
    return np.array(counts)


def noise(rng, extent, scale, most, cuts=(), kind=jnp.bfloat16):
    values = scale * jax.random.normal(rng, extent, jnp.float32)
    if cuts:
        values = values * levels(rng, extent, cuts, -0.22, 0.18)
    return jnp.clip(values, -most, most).astype(kind)


def setup_inputs(seed: int = 0) -> dict:
    key_list = jax.random.split(jax.random.key(seed), 16)
    queries = draw_queries(jax.random.fold_in(key_list[15], 71), 0)
    new_latent = draw_new_latent(jax.random.fold_in(key_list[15], 71), 0)
    cache_pool = noise(key_list[2], (N_ATTN * POOL, LAT + ROPE), 1.0, 6.0, ((0, 4),))
    local_len = jax.vmap(lambda own: ragged(own, REQ_DEV, POOL, MAXLOC, 2))(jax.random.split(key_list[3], N_ATTN)).reshape((N_ATTN, REQ_DEV)).astype(jnp.int32)
    spill_cache = noise(key_list[4], (N_ATTN * SPILL, BLK, LAT + ROPE), 1.0, 6.0, ((0, 4),))
    spill_owner = draw_spill_owner(jax.random.fold_in(key_list[15], 71), 0)
    w_uv = noise(key_list[6], (H, LAT, VH), LAT ** -0.5, 0.25, ((0, 8),))
    w_o = noise(key_list[7], (H * VH, D), (H * VH) ** -0.5, 0.046875, ((0, 8), (1, 4)))
    residual = noise(key_list[8], (TOKENS, D), 0.5, 3.0, ((1, 4),))
    norm_gain = jnp.clip(1.0 + 0.1 * jax.random.normal(key_list[9], (D,), jnp.float32), 0.5, 1.5)
    route_ids_keys = jax.random.split(jax.random.fold_in(key_list[10], 1), TOKENS // (TOKENS // N_REP))
    route_ids_turns = jax.random.permutation(jax.random.fold_in(key_list[10], 3), TOKENS // (TOKENS // N_REP))
    route_ids = jax.vmap(lambda own, number: routed_block(jax.random.fold_in(key_list[10], 2), own, number, TOKENS // N_REP, EXPERTS, TOP, CAPJ, 1))(route_ids_keys, route_ids_turns).reshape((TOKENS, TOP))
    route_scores = jnp.clip(jnp.exp(jax.random.uniform(key_list[11], (TOKENS, TOP), jnp.float32, math.log(0.05), math.log(1.0))), 0.05, 1.0)
    w_gate = noise(key_list[12], (D, EXPERTS * FFE), D ** -0.5, 0.0625, ((1, 16),))
    w_up = noise(key_list[13], (D, EXPERTS * FFE), D ** -0.5, 0.0625, ((1, 16),))
    w_down = noise(key_list[14], (EXPERTS * FFE, D), FFE ** -0.5, 0.125, ((0, 16),))
    return dict(queries=queries, new_latent=new_latent, cache_pool=cache_pool, local_len=local_len, spill_cache=spill_cache, spill_owner=spill_owner, w_uv=w_uv, w_o=w_o, residual=residual, norm_gain=norm_gain, route_ids=route_ids, route_scores=route_scores, w_gate=w_gate, w_up=w_up, w_down=w_down)


floor_score = -1e+30
scale_out = 2.5

def routed_slots(route_ids):
    row_count = TOKENS // N_REP
    route_part = route_ids.reshape(N_REP, row_count, TOP)
    member = jnp.any(route_part[:, :, :, None] == jnp.arange(EXPERTS, dtype=jnp.int32), axis=2)
    order_rank = (jnp.cumsum(member.astype(jnp.int32), axis=1) - 1).astype(jnp.int32)
    slot_ids = jnp.arange(CAPJ, dtype=jnp.int32)
    slot_hit = member[:, None, :, :] & (order_rank[:, None, :, :] == slot_ids[None, :, None, None])
    place_ids = jnp.arange(row_count, dtype=jnp.int32)
    slot_token = lax.optimization_barrier(jnp.sum(jnp.where(slot_hit, place_ids[None, None, :, None], 0), axis=2)).astype(jnp.int32)
    filled = jnp.any(slot_hit, axis=2)
    offsets = (jnp.arange(N_REP, dtype=jnp.int32) * row_count)[:, None, None]
    return (slot_token + offsets, filled)

def reference(queries, new_latent, cache_pool, local_len, spill_cache, spill_owner, w_uv, w_o, residual, norm_gain, route_ids, route_scores, w_gate, w_up, w_down):
    score_scale = float(VH + ROPE) ** (-0.5)
    row_width = LAT + ROPE
    requests = N_ATTN * REQ_DEV
    query_rows = queries.reshape(requests, 2, H, row_width).astype(jnp.float32)
    pools = jnp.concatenate([cache_pool.reshape(N_ATTN, POOL, row_width), jnp.zeros((N_ATTN, MAXLOC, row_width), cache_pool.dtype)], axis=1)
    starts = (jnp.cumsum(local_len, axis=1) - local_len).astype(jnp.int32)

    def device_windows(pool_rows, start_row):
        return jax.vmap(lambda start_one: lax.dynamic_slice_in_dim(pool_rows, start_one, MAXLOC, 0))(start_row)
    windows = jax.vmap(device_windows)(pools, starts).reshape(requests, MAXLOC, row_width).astype(jnp.float32)
    local_scores = jnp.einsum('rthc,rkc->rthk', query_rows, windows) * score_scale
    inside = jnp.arange(MAXLOC, dtype=jnp.int32)[None, :] < local_len.reshape(requests)[:, None]
    local_scores = jnp.where(inside[:, None, None, :], local_scores, floor_score)
    fresh_keys = new_latent.reshape(requests, 2, row_width).astype(jnp.float32)
    fresh_scores = jnp.einsum('rthc,rkc->rthk', query_rows, fresh_keys) * score_scale
    causal = jnp.arange(2)[None, :] <= jnp.arange(2)[:, None]
    fresh_scores = jnp.where(causal[None, :, None, :], fresh_scores, floor_score)
    present = spill_owner >= 0
    owner_ids = jnp.where(present, spill_owner, 0).astype(jnp.int32)
    spill_rows = spill_cache.astype(jnp.float32)
    slot_query = query_rows[owner_ids]
    spill_scores = jnp.einsum('nthc,nbc->nthb', slot_query, spill_rows) * score_scale
    spill_scores = jnp.where(present[:, None, None, None], spill_scores, floor_score)
    row_top = jnp.maximum(lax.optimization_barrier(jnp.max(local_scores, axis=3)), lax.optimization_barrier(jnp.max(fresh_scores, axis=3)))
    row_top = row_top.at[owner_ids].max(lax.optimization_barrier(jnp.max(spill_scores, axis=3)))
    local_weight = jnp.exp(local_scores - row_top[..., None])
    fresh_weight = jnp.exp(fresh_scores - row_top[..., None])
    spill_weight = jnp.exp(spill_scores - row_top[owner_ids][..., None])
    spill_weight = jnp.where(present[:, None, None, None], spill_weight, 0.0)
    denominator = lax.optimization_barrier(jnp.sum(local_weight, axis=3)) + lax.optimization_barrier(jnp.sum(fresh_weight, axis=3))
    denominator = denominator.at[owner_ids].add(lax.optimization_barrier(jnp.sum(spill_weight, axis=3)))
    numerator = jnp.einsum('rthk,rkc->rthc', local_weight.astype(jnp.bfloat16).astype(jnp.float32), windows[:, :, :LAT])
    numerator = numerator + jnp.einsum('rthk,rkc->rthc', fresh_weight.astype(jnp.bfloat16).astype(jnp.float32), fresh_keys[:, :, :LAT])
    spill_numer = jnp.einsum('nthb,nbc->nthc', spill_weight.astype(jnp.bfloat16).astype(jnp.float32), spill_rows[:, :, :LAT])
    numerator = numerator.at[owner_ids].add(spill_numer)
    attended = (numerator / denominator[..., None]).astype(jnp.bfloat16)
    values = jnp.einsum('rthc,hcv->rthv', attended.astype(jnp.float32), w_uv.astype(jnp.float32)).astype(jnp.bfloat16)
    values = values.reshape(TOKENS, H * VH)
    hidden = (residual.astype(jnp.float32) + jnp.dot(values, w_o, preferred_element_type=jnp.float32)).astype(jnp.bfloat16)
    widened = hidden.astype(jnp.float32)
    normed = (widened * lax.rsqrt(lax.optimization_barrier(jnp.mean(widened * widened, axis=1, keepdims=True)) + 1e-06) * norm_gain).astype(jnp.bfloat16)
    share = route_scores / lax.optimization_barrier(jnp.sum(route_scores, axis=1, keepdims=True))
    share_table = lax.optimization_barrier(jnp.sum(jnp.where(route_ids[:, :, None] == jnp.arange(EXPERTS, dtype=jnp.int32), share[:, :, None], 0.0), axis=1))
    slot_token, filled = routed_slots(route_ids)

    def expert_out(expert_index):
        row_ids = slot_token[:, :, expert_index].reshape(-1)
        row_ok = filled[:, :, expert_index].reshape(-1)
        picked = normed[row_ids]
        gate_proj = jnp.dot(picked, lax.dynamic_slice_in_dim(w_gate, expert_index * FFE, FFE, 1), preferred_element_type=jnp.float32)
        up_proj = jnp.dot(picked, lax.dynamic_slice_in_dim(w_up, expert_index * FFE, FFE, 1), preferred_element_type=jnp.float32)
        activated = (jax.nn.silu(gate_proj) * up_proj).astype(jnp.bfloat16)
        result = jnp.dot(activated, lax.dynamic_slice_in_dim(w_down, expert_index * FFE, FFE, 0), preferred_element_type=jnp.float32)
        weight_coef = jnp.where(row_ok, share_table[row_ids, expert_index], 0.0) * scale_out
        return weight_coef[:, None] * result
    outputs = lax.map(expert_out, jnp.arange(EXPERTS, dtype=jnp.int32))
    all_rows = jnp.transpose(slot_token, (2, 0, 1)).reshape(-1)
    routed = jnp.zeros((TOKENS, D), jnp.float32).at[all_rows].add(outputs.reshape(-1, D))
    return (hidden.astype(jnp.float32) + routed).astype(jnp.bfloat16)
```

```python
import jax
import jax.numpy as jnp
from jax import lax
from jax.experimental import pallas as pl
from jax.experimental.pallas import tpu as pltpu
from jax.sharding import PartitionSpec as P

ROPE = 64
VH = 128
EXPERTS = 16
TOP = 4
MAXLOC = 384
CAP = 2


floor_score = -1e30
scale_out = 2.5


def expert_tables(route_ids, part_index, part_count, capacity):
    row_count = route_ids.shape[0] // part_count
    route_part = lax.dynamic_slice_in_dim(route_ids, part_index * row_count, row_count, 0)
    member = jnp.any(
        route_part[:, :, None] == jnp.arange(EXPERTS, dtype=jnp.int32)[None, None, :], axis=1
    )
    order_rank = jnp.cumsum(member.astype(jnp.int32), axis=0) - 1
    slot_ids = jnp.arange(capacity, dtype=jnp.int32)
    slot_hit = member[None, :, :] & (order_rank[None, :, :] == slot_ids[:, None, None])
    place_ids = jnp.arange(row_count, dtype=jnp.int32)
    slot_token = jnp.sum(jnp.where(slot_hit, place_ids[None, :, None], 0), axis=1)
    filled = jnp.any(slot_hit, axis=1)
    return (slot_token.T, filled.T, route_part)


def per_device(
    queries,
    new_latent,
    cache_pool,
    local_len,
    spill_cache,
    spill_owner,
    w_uv,
    w_o,
    residual,
    norm_gain,
    route_ids,
    route_scores,
    w_gate,
    w_up,
    w_down,
):
    n_attn = lax.axis_size("attn")
    n_expert = lax.axis_size("expert")
    n_rep = lax.axis_size("rep")
    attn_here = lax.axis_index("attn")
    expert_here = lax.axis_index("expert")
    rep_here = lax.axis_index("rep")
    req_count = local_len.shape[1]
    head_count = w_uv.shape[0]
    row_width = new_latent.shape[1]
    lat_width = w_uv.shape[1]
    score_scale = float(VH + ROPE) ** (-0.5)
    query_rows = queries.reshape(req_count, 2, head_count, row_width)
    lengths = local_len[0]
    starts = jnp.cumsum(lengths) - lengths
    padded = jnp.concatenate([cache_pool, jnp.zeros((MAXLOC, row_width), cache_pool.dtype)], axis=0)
    windows = jax.vmap(lambda start_one: lax.dynamic_slice_in_dim(padded, start_one, MAXLOC, 0))(
        starts
    )
    local_scores = (
        jnp.einsum("rthc,rkc->rthk", query_rows, windows, preferred_element_type=jnp.float32)
        * score_scale
    )
    inside = jnp.arange(MAXLOC)[None, :] < lengths[:, None]
    local_scores = jnp.where(inside[:, None, None, :], local_scores, floor_score)
    fresh_keys = new_latent.reshape(req_count, 2, row_width)
    fresh_scores = (
        jnp.einsum("rthc,rkc->rthk", query_rows, fresh_keys, preferred_element_type=jnp.float32)
        * score_scale
    )
    causal = jnp.arange(2)[None, :] <= jnp.arange(2)[:, None]
    fresh_scores = jnp.where(causal[None, :, None, :], fresh_scores, floor_score)
    spill_count = spill_cache.shape[0]
    directory = spill_owner.reshape(n_attn, spill_count)
    owner_dev = jnp.where(directory >= 0, directory // req_count, -1)
    earlier = jnp.arange(spill_count)[:, None] > jnp.arange(spill_count)[None, :]
    same_owner = owner_dev[:, :, None] == owner_dev[:, None, :]
    order_rank = jnp.sum(same_owner & earlier[None, :, :], axis=2)
    slot_ids = jnp.arange(CAP)
    own_row = owner_dev[attn_here]
    own_rank = order_rank[attn_here]
    pick_slot = (own_row[None, None, :] == jnp.arange(n_attn)[:, None, None]) & (
        own_rank[None, None, :] == slot_ids[None, :, None]
    )
    outgoing = jnp.einsum(
        "dks,sbc->dkbc",
        pick_slot.astype(jnp.bfloat16),
        spill_cache,
        preferred_element_type=jnp.float32,
    ).astype(jnp.bfloat16)
    incoming = lax.all_to_all(outgoing, "attn", split_axis=0, concat_axis=0, tiled=True)
    mine_slot = (owner_dev[:, None, :] == attn_here) & (
        order_rank[:, None, :] == slot_ids[None, :, None]
    )
    present = jnp.any(mine_slot, axis=2).reshape(-1)
    request = jnp.sum(
        jnp.where(mine_slot, directory[:, None, :] - attn_here * req_count, 0), axis=2
    ).reshape(-1)
    blocks = incoming.reshape(n_attn * CAP, incoming.shape[2], row_width)
    slot_query = jnp.take(query_rows, request, axis=0)
    spill_scores = (
        jnp.einsum("nthc,nbc->nthb", slot_query, blocks, preferred_element_type=jnp.float32)
        * score_scale
    )
    spill_scores = jnp.where(present[:, None, None, None], spill_scores, floor_score)
    belong = (request[None, :] == jnp.arange(req_count)[:, None]) & present[None, :]
    spill_top = jnp.max(
        jnp.where(belong[:, :, None, None], jnp.max(spill_scores, axis=3)[None], floor_score),
        axis=1,
    )
    row_top = jnp.maximum(
        jnp.maximum(jnp.max(local_scores, axis=3), jnp.max(fresh_scores, axis=3)), spill_top
    )
    local_weight = jnp.exp(local_scores - row_top[..., None])
    fresh_weight = jnp.exp(fresh_scores - row_top[..., None])
    spill_weight = jnp.exp(spill_scores - jnp.take(row_top, request, axis=0)[..., None])
    spill_weight = jnp.where(present[:, None, None, None], spill_weight, 0.0)
    belong_f = belong.astype(jnp.float32)
    denominator = jnp.sum(local_weight, axis=3) + jnp.sum(fresh_weight, axis=3)
    denominator = denominator + jnp.einsum(
        "rn,nth->rth", belong_f, jnp.sum(spill_weight, axis=3), precision=lax.Precision.HIGHEST
    )
    numerator = jnp.einsum(
        "rthk,rkc->rthc",
        local_weight.astype(jnp.bfloat16),
        windows[:, :, :lat_width],
        preferred_element_type=jnp.float32,
    )
    numerator = numerator + jnp.einsum(
        "rthk,rkc->rthc",
        fresh_weight.astype(jnp.bfloat16),
        fresh_keys[:, :, :lat_width],
        preferred_element_type=jnp.float32,
    )
    spill_numer = jnp.einsum(
        "nthb,nbc->nthc",
        spill_weight.astype(jnp.bfloat16),
        blocks[:, :, :lat_width],
        preferred_element_type=jnp.float32,
    )
    numerator = numerator + jnp.einsum(
        "rn,nthc->rthc", belong_f, spill_numer, precision=lax.Precision.HIGHEST
    )
    attended = (numerator / denominator[..., None]).astype(jnp.bfloat16)
    values = jnp.einsum(
        "rthc,hcv->rthv", attended, w_uv, preferred_element_type=jnp.float32
    ).astype(jnp.bfloat16)
    values = values.reshape(2 * req_count, head_count * w_uv.shape[2])
    partial_cols = jnp.dot(
        lax.all_gather(values, "attn", axis=0, tiled=True), w_o, preferred_element_type=jnp.float32
    )
    attn_cols = lax.psum(partial_cols.astype(jnp.bfloat16), ("expert", "rep")).astype(jnp.float32)
    hidden_cols = (residual.astype(jnp.float32) + attn_cols).astype(jnp.bfloat16)
    rows_part = route_ids.shape[0] // n_rep
    capacity = rows_part * TOP // EXPERTS * 5 // 4
    shards = n_attn * n_expert // EXPERTS
    slot_token, filled, route_part = expert_tables(route_ids, rep_here, n_rep, capacity)
    part_cols = lax.dynamic_slice_in_dim(hidden_cols, rep_here * rows_part, rows_part, 0)
    dest_expert = (jnp.arange(n_attn) * n_expert + expert_here) // shards
    send_rows = jnp.take(slot_token, dest_expert, axis=0)
    send_ok = jnp.take(filled, dest_expert, axis=0)
    outgoing_rows = jnp.where(
        send_ok[:, :, None], jnp.take(part_cols, send_rows, axis=0), jnp.zeros((), jnp.bfloat16)
    )
    outgoing_rows = outgoing_rows[:, :, None, :]
    received = lax.all_to_all(outgoing_rows, "attn", split_axis=0, concat_axis=2, tiled=True)
    item_count = received.shape[1]
    full_rows = received.reshape(item_count, -1)
    widened = full_rows.astype(jnp.float32)
    normed = (
        widened * lax.rsqrt(jnp.mean(widened * widened, axis=1, keepdims=True) + 1e-06) * norm_gain
    ).astype(jnp.bfloat16)
    gate_proj = jnp.dot(normed, w_gate, preferred_element_type=jnp.float32)
    up_proj = jnp.dot(normed, w_up, preferred_element_type=jnp.float32)
    activated = (jax.nn.silu(gate_proj) * up_proj).astype(jnp.bfloat16)
    result = jnp.dot(activated, w_down, preferred_element_type=jnp.float32)
    returned_block = lax.all_to_all(
        result.reshape(1, item_count, n_attn * n_expert, -1).astype(jnp.bfloat16),
        ("attn", "expert"),
        split_axis=2,
        concat_axis=0,
        tiled=True,
    ).astype(jnp.float32)
    returned = returned_block.reshape(n_attn * n_expert, item_count, -1)
    share_part = lax.dynamic_slice_in_dim(route_scores, rep_here * rows_part, rows_part, 0)
    share_part = share_part / jnp.sum(share_part, axis=1, keepdims=True)
    share_table = jnp.sum(
        jnp.where(
            route_part[:, :, None] == jnp.arange(EXPERTS, dtype=jnp.int32)[None, None, :],
            share_part[:, :, None],
            0.0,
        ),
        axis=1,
    )
    source_expert = jnp.arange(n_attn * n_expert) // shards
    back_rows = jnp.take(slot_token, source_expert, axis=0)
    back_ok = jnp.take(filled, source_expert, axis=0)
    weight_coef = (
        jnp.where(back_ok, share_table[back_rows, source_expert[:, None]], 0.0) * scale_out
    )
    sub_cols = returned.shape[2]
    weighted = (weight_coef[:, :, None] * returned).reshape(-1, sub_cols)
    routed = jax.ops.segment_sum(weighted, back_rows.reshape(-1), num_segments=rows_part)
    own_cols = lax.dynamic_slice_in_dim(part_cols, expert_here * sub_cols, sub_cols, 1)
    return (own_cols.astype(jnp.float32) + routed).astype(jnp.bfloat16)


def remote(src, dst, send_sem, recv_sem, target):
    return pltpu.make_async_remote_copy(
        src_ref=src,
        dst_ref=dst,
        send_sem=send_sem,
        recv_sem=recv_sem,
        device_id=target,
        device_id_type=pl.DeviceIdType.MESH,
    )


def dot_f32(left, right):
    return jnp.dot(left, right, preferred_element_type=jnp.float32)


def layer_kernel(
    q_ref,
    new_ref,
    pool_ref,
    spill_ref,
    pool_req_ref,
    spill_req_ref,
    pick_ref,
    res_ref,
    gain_ref,
    comb_ref,
    comb_t_ref,
    coef_ref,
    uv_hbm,
    wo_hbm,
    gate_hbm,
    up_hbm,
    down_hbm,
    out_ref,
    uv,
    wo,
    gate,
    up,
    down,
    spill_out,
    spill_in,
    value_in,
    part_out,
    part_in,
    row_out,
    row_in,
    normed,
    pair_own,
    pair_out,
    pair_in,
    back_out,
    back_in,
    weight_sem,
    spill_sem,
    value_sem,
    part_sem,
    row_sem,
    pair_row_sem,
    pair_sem,
    back_sem,
):
    n_attn = lax.axis_size("attn")
    n_expert = lax.axis_size("expert")
    a = lax.axis_index("attn")
    e = lax.axis_index("expert")
    r = lax.axis_index("rep")
    other = 1 - r
    me = a * n_expert + e
    plane_me = e * 2 + r
    n_all = n_attn * n_expert
    n_plane = n_expert * 2
    heads = uv.shape[0]
    lat = uv.shape[1]
    width = pool_ref.shape[1]
    score_scale = float(VH + ROPE) ** (-0.5)
    half_units = gate.shape[1]
    width_out = res_ref.shape[1]
    piece = width_out // (2 * n_expert)
    f32 = jnp.float32
    bf16 = jnp.bfloat16

    copies = []

    def fetch(src, dst):
        copy = pltpu.make_async_copy(src, dst, weight_sem.at[len(copies)])
        copy.start()
        copies.append(copy)

    fetch(uv_hbm, uv)
    rows_o = wo.shape[0] // 2
    for i in range(2):
        fetch(wo_hbm.at[pl.ds(i * rows_o, rows_o)], wo.at[pl.ds(i * rows_o, rows_o)])
    cols = pl.ds(pl.multiple_of(r * half_units, 128), half_units)
    rows_g = gate.shape[0] // 4
    for i in range(4):
        span = pl.ds(i * rows_g, rows_g)
        fetch(gate_hbm.at[span, cols], gate.at[span])
        fetch(up_hbm.at[span, cols], up.at[span])
    rows_d = half_units // 4
    for i in range(4):
        begin = pl.multiple_of(r * half_units + i * rows_d, 16)
        fetch(down_hbm.at[pl.ds(begin, rows_d)], down.at[pl.ds(i * rows_d, rows_d)])

    barrier = pltpu.get_barrier_semaphore()
    for step in range(1, n_all):
        dest = lax.rem(me + step, n_all)
        pl.semaphore_signal(
            barrier,
            inc=1,
            device_id=(dest // n_expert, lax.rem(dest, n_expert), r),
            device_id_type=pl.DeviceIdType.MESH,
        )
    for k in range(n_expert):
        pl.semaphore_signal(
            barrier, inc=1, device_id=(a, k, other), device_id_type=pl.DeviceIdType.MESH
        )

    spill_rows = [spill_ref[s].astype(f32) for s in range(spill_ref.shape[0])]
    for d in range(n_attn):
        for k in range(CAP):
            total = pick_ref[d * CAP + k, 0] * spill_rows[0]
            for s in range(1, len(spill_rows)):
                total = total + pick_ref[d * CAP + k, s] * spill_rows[s]
            spill_out[d, k] = total.astype(bf16)
    spill_in[a] = jnp.zeros(spill_in.shape[1:], bf16)
    pl.semaphore_wait(barrier, n_all - 1 + n_expert)

    sends = []
    for step in range(1, n_attn):
        dest = lax.rem(a + step, n_attn)
        copy = remote(
            spill_out.at[dest],
            spill_in.at[a],
            spill_sem.at[0, dest],
            spill_sem.at[1, a],
            (dest, e, r),
        )
        copy.start()
        sends.append(copy)

    q_all = q_ref[...].astype(f32)
    q = jnp.concatenate([q_all[:, h * width : (h + 1) * width] for h in range(heads)], axis=0)
    q = q.astype(bf16)
    n_rows = q.shape[0]
    tokens = q_ref.shape[0]

    def scores(keys):
        return (
            lax.dot_general(q, keys, (((1,), (1,)), ((), ())), preferred_element_type=f32)
            * score_scale
        )

    def row_token(n):
        return lax.rem(lax.broadcasted_iota(jnp.int32, (n_rows, n), 0), tokens)

    pool = pool_ref[...]
    n_pool = pool.shape[0]
    score_pool = jnp.where(
        pool_req_ref[...] == row_token(n_pool) // 2, scores(pool), floor_score
    )
    fresh = new_ref[...]
    token_id = row_token(fresh.shape[0])
    key_id = lax.broadcasted_iota(jnp.int32, token_id.shape, 1)
    fresh_ok = (key_id // 2 == token_id // 2) & (key_id <= token_id)
    score_fresh = jnp.where(fresh_ok, scores(fresh), floor_score)
    for step in range(1, n_attn):
        src = lax.rem(a + step, n_attn)
        remote(
            spill_out.at[src], spill_in.at[src], spill_sem.at[0, src], spill_sem.at[1, src], (src, e, r)
        ).wait_recv()
    spilled = spill_in[...].reshape(-1, width)
    n_spill = spilled.shape[0]
    score_spill = jnp.where(
        spill_req_ref[...] == row_token(n_spill) // 2, scores(spilled), floor_score
    )
    top = jnp.maximum(
        jnp.maximum(
            jnp.max(score_pool, axis=1, keepdims=True), jnp.max(score_fresh, axis=1, keepdims=True)
        ),
        jnp.max(score_spill, axis=1, keepdims=True),
    )
    weight_pool = jnp.exp(score_pool - top)
    weight_fresh = jnp.exp(score_fresh - top)
    weight_spill = jnp.exp(score_spill - top)
    denominator = (
        jnp.sum(weight_pool, axis=1, keepdims=True)
        + jnp.sum(weight_fresh, axis=1, keepdims=True)
        + jnp.sum(weight_spill, axis=1, keepdims=True)
    )
    numerator = (
        dot_f32(weight_pool.astype(bf16), pool[:, :lat])
        + dot_f32(weight_fresh.astype(bf16), fresh[:, :lat])
        + dot_f32(weight_spill.astype(bf16), spilled[:, :lat])
    )
    attended = numerator / denominator
    copies[0].wait()
    half_heads = heads // 2
    sides = []
    for side in range(2):
        sides.append(
            jnp.concatenate(
                [
                    dot_f32(attended[h * tokens : (h + 1) * tokens].astype(bf16), uv[h])
                    for h in range(side * half_heads, (side + 1) * half_heads)
                ],
                axis=1,
            )
        )
    value_in[a] = jnp.concatenate(sides, axis=0).astype(bf16)
    for step in range(1, n_attn):
        dest = lax.rem(a + step, n_attn)
        copy = remote(
            value_in.at[a], value_in.at[a], value_sem.at[0, dest], value_sem.at[1, a], (dest, e, r)
        )
        copy.start()
        sends.append(copy)

    part_rows = res_ref.shape[0] // 2
    res_rows = res_ref[pl.ds(pl.multiple_of(r * part_rows, 16), part_rows), :].astype(f32)
    res_piece = jnp.zeros((2 * part_rows, piece), f32)
    for k in range(n_expert):
        left = res_rows[:, 2 * k * piece : (2 * k + 1) * piece]
        right = res_rows[:, (2 * k + 1) * piece : (2 * k + 2) * piece]
        res_piece = jnp.where(e == k, jnp.concatenate([left, right], axis=0), res_piece)

    for step in range(1, n_attn):
        src = lax.rem(a + step, n_attn)
        remote(
            value_in.at[src], value_in.at[src], value_sem.at[0, src], value_sem.at[1, src], (src, e, r)
        ).wait_recv()
    gathered = [value_in[i].astype(f32) for i in range(n_attn)]
    low = jnp.concatenate([v[:tokens] for v in gathered], axis=0).astype(bf16)
    high = jnp.concatenate([v[tokens:] for v in gathered], axis=0).astype(bf16)
    copies[1].wait()
    copies[2].wait()
    chunk = width_out // 2
    per_chunk = n_expert // 2
    for c in range(2):
        partial = dot_f32(low, wo[:rows_o, c * chunk : (c + 1) * chunk]) + dot_f32(
            high, wo[rows_o:, c * chunk : (c + 1) * chunk]
        )
        for k in range(per_chunk):
            left = partial[:, 2 * k * piece : (2 * k + 1) * piece]
            right = partial[:, (2 * k + 1) * piece : (2 * k + 2) * piece]
            for s in range(2):
                dest_e = c * per_chunk + k
                dest = dest_e * 2 + s
                lo, hi = s * part_rows, (s + 1) * part_rows
                part_out[dest] = jnp.concatenate([left[lo:hi], right[lo:hi]], axis=0).astype(bf16)

                @pl.when(dest != plane_me)
                def _():
                    remote(
                        part_out.at[dest],
                        part_in.at[plane_me],
                        part_sem.at[0, dest],
                        part_sem.at[1, plane_me],
                        (a, dest_e, s),
                    ).start()

    part_in[plane_me] = part_out[plane_me]
    for step in range(1, n_plane):
        src = lax.rem(plane_me + step, n_plane)
        target = (a, src // 2, lax.rem(src, 2))
        copy = remote(
            part_out.at[src], part_in.at[src], part_sem.at[0, src], part_sem.at[1, src], target
        )
        copy.wait_recv()
        sends.append(copy)
    projected = part_in[0].astype(f32)
    for k in range(1, n_plane):
        projected = projected + part_in[k].astype(f32)
    hidden = (res_piece + projected).astype(bf16)

    packed = dot_f32(comb_t_ref[...], hidden).astype(bf16)
    slots = row_out.shape[1]
    for j in range(n_all):
        row_out[j] = packed[j * slots : (j + 1) * slots]
    for step in range(1, n_all):
        dest = lax.rem(me + step, n_all)
        target = (dest // n_expert, lax.rem(dest, n_expert), r)
        copy = remote(
            row_out.at[dest], row_in.at[r, me], row_sem.at[0, dest], row_sem.at[1, me], target
        )
        copy.start()
        sends.append(copy)
    row_in[r, me] = row_out[me]
    for step in range(1, n_all):
        src = lax.rem(me + step, n_all)
        target = (src // n_expert, lax.rem(src, n_expert), r)
        remote(
            row_out.at[src], row_in.at[r, src], row_sem.at[0, src], row_sem.at[1, src], target
        ).wait_recv()
    pair_rows = remote(
        row_in.at[r], row_in.at[r], pair_row_sem.at[0], pair_row_sem.at[1], (a, e, other)
    )
    pair_rows.start()
    sends.append(pair_rows)
    remote(
        row_in.at[other], row_in.at[other], pair_row_sem.at[0], pair_row_sem.at[1], (a, e, other)
    ).wait_recv()

    half_slots = slots // 2

    def expert_rows(k):
        first = row_in[0, k].astype(f32)
        second = row_in[1, k].astype(f32)
        return (
            jnp.concatenate([first[:half_slots], second[:half_slots]], axis=0),
            jnp.concatenate([first[half_slots:], second[half_slots:]], axis=0),
        )

    squares = jnp.zeros((slots, piece), f32)
    for k in range(n_all):
        left, right = expert_rows(k)
        squares = squares + left * left + right * right
    mean = jnp.sum(squares, axis=1, keepdims=True) / float(2 * n_all * piece)
    inverse = lax.rsqrt(mean + 1e-06)
    for k in range(n_all):
        left, right = expert_rows(k)
        normed[2 * k] = (left * inverse * gain_ref[2 * k]).astype(bf16)
        normed[2 * k + 1] = (right * inverse * gain_ref[2 * k + 1]).astype(bf16)

    for i in range(8):
        copies[3 + i].wait()

    def gate_step(k, carry):
        gate_sum, up_sum = carry
        rows = normed[k]
        span = pl.ds(pl.multiple_of(k * piece, 16), piece)
        return (gate_sum + dot_f32(rows, gate[span, :]), up_sum + dot_f32(rows, up[span, :]))

    zeros = jnp.zeros((slots, half_units), f32)
    gate_sum, up_sum = lax.fori_loop(0, 2 * n_all, gate_step, (zeros, zeros))
    activated = (gate_sum / (1.0 + jnp.exp(-gate_sum)) * up_sum).astype(bf16)
    for i in range(4):
        copies[11 + i].wait()

    coef = coef_ref[...]
    n_chunk = n_all // 2
    span_d = 4 * piece

    def down_chunk(i):
        return lax.rem(me // 2 + 1 + i, n_chunk)

    def pair_copy(c):
        return remote(
            pair_out.at[c], pair_in.at[c], pair_sem.at[0, c], pair_sem.at[1, c], (a, e, other)
        )

    def back_copy(dest):
        target = (dest // n_expert, lax.rem(dest, n_expert), r)
        return remote(
            back_out.at[dest], back_in.at[me], back_sem.at[0, dest], back_sem.at[1, me], target
        )

    def send_back(c):
        pair_copy(c).wait_recv()
        both = pair_own[c] + pair_in[c]
        for p in range(2):
            dest = 2 * c + p
            left = both[:, 2 * p * piece : (2 * p + 1) * piece]
            right = both[:, (2 * p + 1) * piece : (2 * p + 2) * piece]
            back_out[dest] = jnp.concatenate([left, right], axis=0).astype(bf16)

            @pl.when(dest != me)
            def _():
                back_copy(dest).start()

    for i in range(n_chunk):
        c = down_chunk(i)
        result = dot_f32(activated, down[:, pl.ds(pl.multiple_of(c * span_d, 128), span_d)]) * coef
        upper, lower = result[:half_slots], result[half_slots:]
        pair_own[c] = jnp.where(r == 0, upper, lower)
        pair_out[c] = jnp.where(r == 0, lower, upper)
        pair_copy(c).start()
        if i > 0:
            send_back(down_chunk(i - 1))
    send_back(down_chunk(n_chunk - 1))
    back_in[me] = back_out[me]
    for step in range(1, n_all):
        src = lax.rem(me + step, n_all)
        target = (src // n_expert, lax.rem(src, n_expert), r)
        copy = remote(
            back_out.at[src], back_in.at[src], back_sem.at[0, src], back_sem.at[1, src], target
        )
        copy.wait_recv()
        sends.append(copy)
    returned = back_in[...].reshape(-1, piece)
    routed = dot_f32(comb_ref[...], returned)
    out_ref[...] = (hidden.astype(f32) + routed).astype(bf16)
    for i in range(n_chunk):
        pair_copy(i).wait_send()
    for copy in sends:
        copy.wait_send()


def fused_device(
    queries,
    new_latent,
    cache_pool,
    local_len,
    spill_cache,
    spill_owner,
    w_uv,
    w_o,
    residual,
    norm_gain,
    route_ids,
    route_scores,
    w_gate,
    w_up,
    w_down,
):
    n_attn = lax.axis_size("attn")
    n_expert = lax.axis_size("expert")
    n_rep = lax.axis_size("rep")
    a = lax.axis_index("attn")
    me = a * n_expert + lax.axis_index("expert")
    r = lax.axis_index("rep")
    n_all = n_attn * n_expert
    req_count = local_len.shape[1]
    width = new_latent.shape[1]
    pool_rows = cache_pool.shape[0]
    piece = w_down.shape[1] // (2 * n_all)
    half_units = w_gate.shape[1] // n_rep
    rows_part = route_ids.shape[0] // n_rep
    slots = 8

    place = jnp.arange(pool_rows, dtype=jnp.int32)
    before = jnp.arange(req_count)[:, None] >= jnp.arange(req_count)[None, :]
    ends = jnp.sum(jnp.where(before, local_len[0][None, :], 0), axis=1)
    pool_req = jnp.sum((place[None, :] >= ends[:, None]).astype(jnp.int32), axis=0)[None, :]

    spill_count = spill_cache.shape[0]
    directory = spill_owner.reshape(n_attn, spill_count)
    owner_dev = jnp.where(directory >= 0, directory // req_count, -1)
    earlier = jnp.arange(spill_count)[:, None] > jnp.arange(spill_count)[None, :]
    same_owner = owner_dev[:, :, None] == owner_dev[:, None, :]
    order_rank = jnp.sum(same_owner & earlier[None, :, :], axis=2)
    slot_ids = jnp.arange(CAP)
    own = jnp.arange(n_attn)[:, None] == a
    own_row = jnp.sum(jnp.where(own, owner_dev, 0), axis=0)
    own_rank = jnp.sum(jnp.where(own, order_rank, 0), axis=0)
    pick = (own_row[None, None, :] == jnp.arange(n_attn)[:, None, None]) & (
        own_rank[None, None, :] == slot_ids[None, :, None]
    )
    pick = pick.astype(jnp.float32).reshape(n_attn * CAP, spill_count)
    mine = (owner_dev[:, None, :] == a) & (order_rank[:, None, :] == slot_ids[None, :, None])
    spill_req = (
        jnp.sum(jnp.where(mine, directory[:, None, :] - a * req_count + 1, 0), axis=2) - 1
    )
    block = spill_cache.shape[1]
    spill_req = jnp.broadcast_to(spill_req.reshape(-1, 1), (n_attn * CAP, block)).reshape(1, -1)

    experts = jnp.arange(EXPERTS, dtype=jnp.int32)
    named = route_ids[:, :, None] == experts[None, None, :]
    member = jnp.any(named, axis=1).reshape(n_rep, rows_part, EXPERTS)
    share = route_scores / jnp.sum(route_scores, axis=1, keepdims=True)
    share_table = jnp.sum(jnp.where(named, share[:, :, None], 0.0), axis=1)
    share_table = share_table.reshape(n_rep, rows_part, EXPERTS)
    row_before = jnp.arange(rows_part)[:, None] > jnp.arange(rows_part)[None, :]
    rank = jnp.sum(member[:, None, :, :] & row_before[None, :, :, None], axis=2)
    chosen = member[:, :, :, None] & (rank[:, :, :, None] == jnp.arange(slots))
    at_expert = experts == me
    coef = jnp.sum(
        jnp.where(
            chosen & at_expert[None, None, :, None], share_table[:, :, :, None] * scale_out, 0.0
        ),
        axis=(1, 2),
    ).reshape(n_rep * slots, 1)
    at_rep = (jnp.arange(n_rep) == r)[:, None, None, None]
    chosen_here = jnp.any(chosen & at_rep, axis=0)
    two = jnp.arange(2)
    comb = (
        chosen_here[None, :, :, None, :]
        & (two[:, None, None, None, None] == two[None, None, None, :, None])
    ).astype(jnp.bfloat16)
    comb = comb.reshape(2 * rows_part, n_all * 2 * slots)
    gain = norm_gain.reshape(2 * n_all, 1, piece)

    vmem = pl.BlockSpec(memory_space=pltpu.VMEM)
    smem = pl.BlockSpec(memory_space=pltpu.SMEM)
    hbm = pl.BlockSpec(memory_space=pl.ANY)
    bf16 = jnp.bfloat16
    n_plane = n_expert * n_rep
    dma = pltpu.SemaphoreType.DMA
    tokens = queries.shape[0]
    value_width = w_uv.shape[0] * w_uv.shape[2] // 2
    out = pl.pallas_call(
        layer_kernel,
        out_shape=jax.ShapeDtypeStruct((2 * rows_part, piece), bf16),
        in_specs=[vmem] * 6 + [smem] + [vmem] * 5 + [hbm] * 5,
        out_specs=vmem,
        scratch_shapes=[
            pltpu.VMEM(w_uv.shape, bf16),
            pltpu.VMEM(w_o.shape, bf16),
            pltpu.VMEM((w_gate.shape[0], half_units), bf16),
            pltpu.VMEM((w_up.shape[0], half_units), bf16),
            pltpu.VMEM((half_units, w_down.shape[1]), bf16),
            pltpu.VMEM((n_attn, CAP, block, width), bf16),
            pltpu.VMEM((n_attn, CAP, block, width), bf16),
            pltpu.VMEM((n_attn, 2 * tokens, value_width), bf16),
            pltpu.VMEM((n_plane, 2 * rows_part, piece), bf16),
            pltpu.VMEM((n_plane, 2 * rows_part, piece), bf16),
            pltpu.VMEM((n_all, 2 * slots, piece), bf16),
            pltpu.VMEM((n_rep, n_all, 2 * slots, piece), bf16),
            pltpu.VMEM((2 * n_all, 2 * slots, piece), bf16),
            pltpu.VMEM((n_all // 2, slots, 4 * piece), jnp.float32),
            pltpu.VMEM((n_all // 2, slots, 4 * piece), jnp.float32),
            pltpu.VMEM((n_all // 2, slots, 4 * piece), jnp.float32),
            pltpu.VMEM((n_all, 2 * slots, piece), bf16),
            pltpu.VMEM((n_all, 2 * slots, piece), bf16),
            dma((15,)),
            dma((2, n_attn)),
            dma((2, n_attn)),
            dma((2, n_plane)),
            dma((2, n_all)),
            dma((2,)),
            dma((2, n_all // 2)),
            dma((2, n_all)),
        ],
        compiler_params=pltpu.CompilerParams(
            collective_id=0, has_side_effects=True, vmem_limit_bytes=60 * 1024 * 1024
        ),
    )(
        queries,
        new_latent,
        cache_pool,
        spill_cache,
        pool_req,
        spill_req,
        pick,
        residual,
        gain,
        comb,
        comb.T,
        coef,
        w_uv,
        w_o,
        w_gate,
        w_up,
        w_down,
    )
    return jnp.concatenate([out[:rows_part], out[rows_part:]], axis=1)


def solution(mesh):
    n_attn, n_expert, n_rep = (mesh.shape[name] for name in ("attn", "expert", "rep"))
    fused = n_attn * n_expert == EXPERTS and n_attn == 4 and n_rep == 2
    return jax.shard_map(
        fused_device if fused else per_device,
        mesh=mesh,
        in_specs=(
            P("attn", ("expert", "rep")),
            P("attn", None),
            P("attn", None),
            P("attn", None),
            P("attn", None, None),
            P(),
            P(("expert", "rep"), None, None),
            P(("expert", "rep"), "attn"),
            P(None, "attn"),
            P(),
            P(),
            P(),
            P(None, ("attn", "expert")),
            P(None, ("attn", "expert")),
            P(("attn", "expert"), None),
        ),
        out_specs=P("rep", ("attn", "expert")),
        check_vma=False,
    )
```

```python
import jax
import jax.numpy as jnp
from jax import lax
from jax.experimental import pallas as pl
from jax.experimental.pallas import tpu as pltpu
from jax.sharding import PartitionSpec as P

ROPE = 64
VH = 128
EXPERTS = 16
TOP = 4
MAXLOC = 384
CAP = 2


floor_score = -1e30
scale_out = 2.5


def expert_tables(route_ids, part_index, part_count, capacity):
    row_count = route_ids.shape[0] // part_count
    route_part = lax.dynamic_slice_in_dim(route_ids, part_index * row_count, row_count, 0)
    member = jnp.any(
        route_part[:, :, None] == jnp.arange(EXPERTS, dtype=jnp.int32)[None, None, :], axis=1
    )
    order_rank = jnp.cumsum(member.astype(jnp.int32), axis=0) - 1
    slot_ids = jnp.arange(capacity, dtype=jnp.int32)
    slot_hit = member[None, :, :] & (order_rank[None, :, :] == slot_ids[:, None, None])
    place_ids = jnp.arange(row_count, dtype=jnp.int32)
    slot_token = jnp.sum(jnp.where(slot_hit, place_ids[None, :, None], 0), axis=1)
    filled = jnp.any(slot_hit, axis=1)
    return (slot_token.T, filled.T, route_part)


def per_device(
    queries,
    new_latent,
    cache_pool,
    local_len,
    spill_cache,
    spill_owner,
    w_uv,
    w_o,
    residual,
    norm_gain,
    route_ids,
    route_scores,
    w_gate,
    w_up,
    w_down,
):
    n_attn = lax.axis_size("attn")
    n_expert = lax.axis_size("expert")
    n_rep = lax.axis_size("rep")
    attn_here = lax.axis_index("attn")
    expert_here = lax.axis_index("expert")
    rep_here = lax.axis_index("rep")
    req_count = local_len.shape[1]
    head_count = w_uv.shape[0]
    row_width = new_latent.shape[1]
    lat_width = w_uv.shape[1]
    score_scale = float(VH + ROPE) ** (-0.5)
    query_rows = queries.reshape(req_count, 2, head_count, row_width)
    lengths = local_len[0]
    starts = jnp.cumsum(lengths) - lengths
    padded = jnp.concatenate([cache_pool, jnp.zeros((MAXLOC, row_width), cache_pool.dtype)], axis=0)
    windows = jax.vmap(lambda start_one: lax.dynamic_slice_in_dim(padded, start_one, MAXLOC, 0))(
        starts
    )
    local_scores = (
        jnp.einsum("rthc,rkc->rthk", query_rows, windows, preferred_element_type=jnp.float32)
        * score_scale
    )
    inside = jnp.arange(MAXLOC)[None, :] < lengths[:, None]
    local_scores = jnp.where(inside[:, None, None, :], local_scores, floor_score)
    fresh_keys = new_latent.reshape(req_count, 2, row_width)
    fresh_scores = (
        jnp.einsum("rthc,rkc->rthk", query_rows, fresh_keys, preferred_element_type=jnp.float32)
        * score_scale
    )
    causal = jnp.arange(2)[None, :] <= jnp.arange(2)[:, None]
    fresh_scores = jnp.where(causal[None, :, None, :], fresh_scores, floor_score)
    spill_count = spill_cache.shape[0]
    directory = spill_owner.reshape(n_attn, spill_count)
    owner_dev = jnp.where(directory >= 0, directory // req_count, -1)
    earlier = jnp.arange(spill_count)[:, None] > jnp.arange(spill_count)[None, :]
    same_owner = owner_dev[:, :, None] == owner_dev[:, None, :]
    order_rank = jnp.sum(same_owner & earlier[None, :, :], axis=2)
    slot_ids = jnp.arange(CAP)
    own_row = owner_dev[attn_here]
    own_rank = order_rank[attn_here]
    pick_slot = (own_row[None, None, :] == jnp.arange(n_attn)[:, None, None]) & (
        own_rank[None, None, :] == slot_ids[None, :, None]
    )
    outgoing = jnp.einsum(
        "dks,sbc->dkbc",
        pick_slot.astype(jnp.bfloat16),
        spill_cache,
        preferred_element_type=jnp.float32,
    ).astype(jnp.bfloat16)
    incoming = lax.all_to_all(outgoing, "attn", split_axis=0, concat_axis=0, tiled=True)
    mine_slot = (owner_dev[:, None, :] == attn_here) & (
        order_rank[:, None, :] == slot_ids[None, :, None]
    )
    present = jnp.any(mine_slot, axis=2).reshape(-1)
    request = jnp.sum(
        jnp.where(mine_slot, directory[:, None, :] - attn_here * req_count, 0), axis=2
    ).reshape(-1)
    blocks = incoming.reshape(n_attn * CAP, incoming.shape[2], row_width)
    slot_query = jnp.take(query_rows, request, axis=0)
    spill_scores = (
        jnp.einsum("nthc,nbc->nthb", slot_query, blocks, preferred_element_type=jnp.float32)
        * score_scale
    )
    spill_scores = jnp.where(present[:, None, None, None], spill_scores, floor_score)
    belong = (request[None, :] == jnp.arange(req_count)[:, None]) & present[None, :]
    spill_top = jnp.max(
        jnp.where(belong[:, :, None, None], jnp.max(spill_scores, axis=3)[None], floor_score),
        axis=1,
    )
    row_top = jnp.maximum(
        jnp.maximum(jnp.max(local_scores, axis=3), jnp.max(fresh_scores, axis=3)), spill_top
    )
    local_weight = jnp.exp(local_scores - row_top[..., None])
    fresh_weight = jnp.exp(fresh_scores - row_top[..., None])
    spill_weight = jnp.exp(spill_scores - jnp.take(row_top, request, axis=0)[..., None])
    spill_weight = jnp.where(present[:, None, None, None], spill_weight, 0.0)
    belong_f = belong.astype(jnp.float32)
    denominator = jnp.sum(local_weight, axis=3) + jnp.sum(fresh_weight, axis=3)
    denominator = denominator + jnp.einsum(
        "rn,nth->rth", belong_f, jnp.sum(spill_weight, axis=3), precision=lax.Precision.HIGHEST
    )
    numerator = jnp.einsum(
        "rthk,rkc->rthc",
        local_weight.astype(jnp.bfloat16),
        windows[:, :, :lat_width],
        preferred_element_type=jnp.float32,
    )
    numerator = numerator + jnp.einsum(
        "rthk,rkc->rthc",
        fresh_weight.astype(jnp.bfloat16),
        fresh_keys[:, :, :lat_width],
        preferred_element_type=jnp.float32,
    )
    spill_numer = jnp.einsum(
        "nthb,nbc->nthc",
        spill_weight.astype(jnp.bfloat16),
        blocks[:, :, :lat_width],
        preferred_element_type=jnp.float32,
    )
    numerator = numerator + jnp.einsum(
        "rn,nthc->rthc", belong_f, spill_numer, precision=lax.Precision.HIGHEST
    )
    attended = (numerator / denominator[..., None]).astype(jnp.bfloat16)
    values = jnp.einsum(
        "rthc,hcv->rthv", attended, w_uv, preferred_element_type=jnp.float32
    ).astype(jnp.bfloat16)
    values = values.reshape(2 * req_count, head_count * w_uv.shape[2])
    partial_cols = jnp.dot(
        lax.all_gather(values, "attn", axis=0, tiled=True), w_o, preferred_element_type=jnp.float32
    )
    attn_cols = lax.psum(partial_cols.astype(jnp.bfloat16), ("expert", "rep")).astype(jnp.float32)
    hidden_cols = (residual.astype(jnp.float32) + attn_cols).astype(jnp.bfloat16)
    rows_part = route_ids.shape[0] // n_rep
    capacity = rows_part * TOP // EXPERTS * 5 // 4
    shards = n_attn * n_expert // EXPERTS
    slot_token, filled, route_part = expert_tables(route_ids, rep_here, n_rep, capacity)
    part_cols = lax.dynamic_slice_in_dim(hidden_cols, rep_here * rows_part, rows_part, 0)
    dest_expert = (jnp.arange(n_attn) * n_expert + expert_here) // shards
    send_rows = jnp.take(slot_token, dest_expert, axis=0)
    send_ok = jnp.take(filled, dest_expert, axis=0)
    outgoing_rows = jnp.where(
        send_ok[:, :, None], jnp.take(part_cols, send_rows, axis=0), jnp.zeros((), jnp.bfloat16)
    )
    outgoing_rows = outgoing_rows[:, :, None, :]
    received = lax.all_to_all(outgoing_rows, "attn", split_axis=0, concat_axis=2, tiled=True)
    item_count = received.shape[1]
    full_rows = received.reshape(item_count, -1)
    widened = full_rows.astype(jnp.float32)
    normed = (
        widened * lax.rsqrt(jnp.mean(widened * widened, axis=1, keepdims=True) + 1e-06) * norm_gain
    ).astype(jnp.bfloat16)
    gate_proj = jnp.dot(normed, w_gate, preferred_element_type=jnp.float32)
    up_proj = jnp.dot(normed, w_up, preferred_element_type=jnp.float32)
    activated = (jax.nn.silu(gate_proj) * up_proj).astype(jnp.bfloat16)
    result = jnp.dot(activated, w_down, preferred_element_type=jnp.float32)
    returned_block = lax.all_to_all(
        result.reshape(1, item_count, n_attn * n_expert, -1).astype(jnp.bfloat16),
        ("attn", "expert"),
        split_axis=2,
        concat_axis=0,
        tiled=True,
    ).astype(jnp.float32)
    returned = returned_block.reshape(n_attn * n_expert, item_count, -1)
    share_part = lax.dynamic_slice_in_dim(route_scores, rep_here * rows_part, rows_part, 0)
    share_part = share_part / jnp.sum(share_part, axis=1, keepdims=True)
    share_table = jnp.sum(
        jnp.where(
            route_part[:, :, None] == jnp.arange(EXPERTS, dtype=jnp.int32)[None, None, :],
            share_part[:, :, None],
            0.0,
        ),
        axis=1,
    )
    source_expert = jnp.arange(n_attn * n_expert) // shards
    back_rows = jnp.take(slot_token, source_expert, axis=0)
    back_ok = jnp.take(filled, source_expert, axis=0)
    weight_coef = (
        jnp.where(back_ok, share_table[back_rows, source_expert[:, None]], 0.0) * scale_out
    )
    sub_cols = returned.shape[2]
    weighted = (weight_coef[:, :, None] * returned).reshape(-1, sub_cols)
    routed = jax.ops.segment_sum(weighted, back_rows.reshape(-1), num_segments=rows_part)
    own_cols = lax.dynamic_slice_in_dim(part_cols, expert_here * sub_cols, sub_cols, 1)
    return (own_cols.astype(jnp.float32) + routed).astype(jnp.bfloat16)


def remote(src, dst, send_sem, recv_sem, target):
    return pltpu.make_async_remote_copy(
        src_ref=src,
        dst_ref=dst,
        send_sem=send_sem,
        recv_sem=recv_sem,
        device_id=target,
        device_id_type=pl.DeviceIdType.MESH,
    )


def dot_f32(left, right):
    return jnp.dot(left, right, preferred_element_type=jnp.float32)


def layer_kernel(
    q_ref,
    new_ref,
    pool_ref,
    spill_ref,
    len_ref,
    owner_ref,
    res_ref,
    gain_ref,
    ids_ref,
    scores_ref,
    uv_hbm,
    wo_hbm,
    gate_hbm,
    up_hbm,
    down_hbm,
    out_ref,
    uv,
    wo,
    gate,
    up,
    down,
    spill_out,
    spill_in,
    value_in,
    part_out,
    part_in,
    row_out,
    row_in,
    normed,
    pair_own,
    pair_out,
    pair_in,
    back_out,
    back_in,
    weight_sem,
    spill_sem,
    value_sem,
    part_sem,
    row_sem,
    pair_row_sem,
    pair_sem,
    back_sem,
):
    n_attn = lax.axis_size("attn")
    n_expert = lax.axis_size("expert")
    a = lax.axis_index("attn")
    e = lax.axis_index("expert")
    r = lax.axis_index("rep")
    other = 1 - r
    me = a * n_expert + e
    plane_me = e * 2 + r
    n_all = n_attn * n_expert
    n_plane = n_expert * 2
    heads = uv.shape[0]
    lat = uv.shape[1]
    width = pool_ref.shape[1]
    score_scale = float(VH + ROPE) ** (-0.5)
    half_units = gate.shape[1]
    width_out = res_ref.shape[1]
    piece = width_out // (2 * n_expert)
    f32 = jnp.float32
    bf16 = jnp.bfloat16

    copies = []

    def fetch(src, dst):
        copy = pltpu.make_async_copy(src, dst, weight_sem.at[len(copies)])
        copy.start()
        copies.append(copy)

    fetch(uv_hbm, uv)
    rows_o = wo.shape[0] // 2
    for i in range(2):
        fetch(wo_hbm.at[pl.ds(i * rows_o, rows_o)], wo.at[pl.ds(i * rows_o, rows_o)])
    cols = pl.ds(pl.multiple_of(r * half_units, 128), half_units)
    rows_g = gate.shape[0] // 4
    for i in range(4):
        span = pl.ds(i * rows_g, rows_g)
        fetch(gate_hbm.at[span, cols], gate.at[span])
        fetch(up_hbm.at[span, cols], up.at[span])
    rows_d = half_units // 4
    for i in range(4):
        begin = pl.multiple_of(r * half_units + i * rows_d, 16)
        fetch(down_hbm.at[pl.ds(begin, rows_d)], down.at[pl.ds(i * rows_d, rows_d)])

    barrier = pltpu.get_barrier_semaphore()
    for step in range(1, n_all):
        dest = lax.rem(me + step, n_all)
        pl.semaphore_signal(
            barrier,
            inc=1,
            device_id=(dest // n_expert, lax.rem(dest, n_expert), r),
            device_id_type=pl.DeviceIdType.MESH,
        )
    for k in range(n_expert):
        pl.semaphore_signal(
            barrier, inc=1, device_id=(a, k, other), device_id_type=pl.DeviceIdType.MESH
        )

    spill_rows = [spill_ref[s].astype(f32) for s in range(spill_ref.shape[0])]
    n_slots = len(spill_rows)
    req_count = len_ref.shape[1]
    own = [owner_ref[a * n_slots + s] for s in range(n_slots)]
    for d in range(n_attn):
        totals = [jnp.zeros(spill_rows[0].shape, f32) for k in range(CAP)]
        count = jnp.int32(0)
        for s in range(n_slots):
            to_d = (own[s] >= d * req_count) & (own[s] < (d + 1) * req_count)
            for k in range(CAP):
                factor = jnp.where(to_d & (count == k), 1.0, 0.0)
                totals[k] = totals[k] + factor * spill_rows[s]
            count = count + jnp.where(to_d, 1, 0)
        for k in range(CAP):
            spill_out[d, k] = totals[k].astype(bf16)
    spill_in[a] = jnp.zeros(spill_in.shape[1:], bf16)
    pl.semaphore_wait(barrier, n_all - 1 + n_expert)

    sends = []
    for step in range(1, n_attn):
        dest = lax.rem(a + step, n_attn)
        copy = remote(
            spill_out.at[dest],
            spill_in.at[a],
            spill_sem.at[0, dest],
            spill_sem.at[1, a],
            (dest, e, r),
        )
        copy.start()
        sends.append(copy)

    q_all = q_ref[...].astype(f32)
    q = jnp.concatenate([q_all[:, h * width : (h + 1) * width] for h in range(heads)], axis=0)
    q = q.astype(bf16)
    n_rows = q.shape[0]
    tokens = q_ref.shape[0]

    def scores(keys):
        return (
            lax.dot_general(q, keys, (((1,), (1,)), ((), ())), preferred_element_type=f32)
            * score_scale
        )

    def row_token(n):
        return lax.rem(lax.broadcasted_iota(jnp.int32, (n_rows, n), 0), tokens)

    pool = pool_ref[...]
    n_pool = pool.shape[0]
    place = lax.broadcasted_iota(jnp.int32, (1, n_pool), 1)
    pool_req = jnp.zeros((1, n_pool), jnp.int32)
    end = jnp.int32(0)
    for k in range(req_count):
        end = end + len_ref[0, k]
        pool_req = pool_req + jnp.where(place >= end, 1, 0)
    block = spill_ref.shape[1]
    column = lax.broadcasted_iota(jnp.int32, (1, n_attn * CAP * block), 1) // block
    spill_req = jnp.full(column.shape, -1, jnp.int32)
    for src in range(n_attn):
        count = jnp.int32(0)
        for s in range(n_slots):
            request = owner_ref[src * n_slots + s] - a * req_count
            mine = (request >= 0) & (request < req_count)
            slot = jnp.where(mine & (count < CAP), src * CAP + count, -1)
            spill_req = jnp.where(column == slot, request, spill_req)
            count = count + jnp.where(mine, 1, 0)
    score_pool = jnp.where(
        pool_req == row_token(n_pool) // 2, scores(pool), floor_score
    )
    fresh = new_ref[...]
    token_id = row_token(fresh.shape[0])
    key_id = lax.broadcasted_iota(jnp.int32, token_id.shape, 1)
    fresh_ok = (key_id // 2 == token_id // 2) & (key_id <= token_id)
    score_fresh = jnp.where(fresh_ok, scores(fresh), floor_score)
    for step in range(1, n_attn):
        src = lax.rem(a + step, n_attn)
        remote(
            spill_out.at[src], spill_in.at[src], spill_sem.at[0, src], spill_sem.at[1, src], (src, e, r)
        ).wait_recv()
    spilled = spill_in[...].reshape(-1, width)
    n_spill = spilled.shape[0]
    score_spill = jnp.where(
        spill_req == row_token(n_spill) // 2, scores(spilled), floor_score
    )
    top = jnp.maximum(
        jnp.maximum(
            jnp.max(score_pool, axis=1, keepdims=True), jnp.max(score_fresh, axis=1, keepdims=True)
        ),
        jnp.max(score_spill, axis=1, keepdims=True),
    )
    weight_pool = jnp.exp(score_pool - top)
    weight_fresh = jnp.exp(score_fresh - top)
    weight_spill = jnp.exp(score_spill - top)
    denominator = (
        jnp.sum(weight_pool, axis=1, keepdims=True)
        + jnp.sum(weight_fresh, axis=1, keepdims=True)
        + jnp.sum(weight_spill, axis=1, keepdims=True)
    )
    numerator = (
        dot_f32(weight_pool.astype(bf16), pool[:, :lat])
        + dot_f32(weight_fresh.astype(bf16), fresh[:, :lat])
        + dot_f32(weight_spill.astype(bf16), spilled[:, :lat])
    )
    attended = numerator / denominator
    copies[0].wait()
    half_heads = heads // 2
    sides = []
    for side in range(2):
        sides.append(
            jnp.concatenate(
                [
                    dot_f32(attended[h * tokens : (h + 1) * tokens].astype(bf16), uv[h])
                    for h in range(side * half_heads, (side + 1) * half_heads)
                ],
                axis=1,
            )
        )
    value_in[a] = jnp.concatenate(sides, axis=0).astype(bf16)
    for step in range(1, n_attn):
        dest = lax.rem(a + step, n_attn)
        copy = remote(
            value_in.at[a], value_in.at[a], value_sem.at[0, dest], value_sem.at[1, a], (dest, e, r)
        )
        copy.start()
        sends.append(copy)

    part_rows = res_ref.shape[0] // 2
    res_rows = res_ref[pl.ds(pl.multiple_of(r * part_rows, 16), part_rows), :].astype(f32)
    res_piece = jnp.zeros((2 * part_rows, piece), f32)
    for k in range(n_expert):
        left = res_rows[:, 2 * k * piece : (2 * k + 1) * piece]
        right = res_rows[:, (2 * k + 1) * piece : (2 * k + 2) * piece]
        res_piece = jnp.where(e == k, jnp.concatenate([left, right], axis=0), res_piece)

    slots = row_out.shape[1]
    half_slots = slots // 2
    ids = ids_ref[...]
    n_tok = ids.shape[0]
    share = scores_ref[...]
    share = share / jnp.sum(share, axis=1, keepdims=True)
    expert_id = lax.broadcasted_iota(jnp.int32, (n_tok, n_all), 1)
    member = jnp.zeros((n_tok, n_all), f32)
    share_table = jnp.zeros((n_tok, n_all), f32)
    for k in range(TOP):
        hit = ids[:, k : k + 1] == expert_id
        member = member + jnp.where(hit, 1.0, 0.0)
        share_table = share_table + jnp.where(hit, share[:, k : k + 1], 0.0)
    t0 = lax.broadcasted_iota(jnp.int32, (n_tok, n_tok), 0)
    t1 = lax.broadcasted_iota(jnp.int32, (n_tok, n_tok), 1)
    earlier = jnp.where((t0 > t1) & (t0 // part_rows == t1 // part_rows), 1.0, 0.0)
    rank = dot_f32(earlier.astype(bf16), member.astype(bf16))
    member_here = jnp.where(r == 0, member[:part_rows], member[part_rows:])
    rank_here = jnp.where(r == 0, rank[:part_rows], rank[part_rows:])
    n_cols = n_all * slots
    spread = jnp.where(
        lax.broadcasted_iota(jnp.int32, (n_all, n_cols), 1) // slots
        == lax.broadcasted_iota(jnp.int32, (n_all, n_cols), 0),
        1.0,
        0.0,
    ).astype(bf16)
    col_id = lax.broadcasted_iota(jnp.int32, (part_rows, n_cols), 1)
    col_slot = lax.rem(col_id, half_slots).astype(f32)
    chosen = (dot_f32(member_here.astype(bf16), spread) > 0.5) & (
        dot_f32(rank_here.astype(bf16), spread) == col_slot
    )
    col_half = lax.rem(col_id // half_slots, 2)
    comb = jnp.concatenate(
        [jnp.where(chosen & (col_half == half), 1.0, 0.0) for half in range(2)], axis=0
    )
    comb_t = comb.T.astype(bf16)
    comb = comb.astype(bf16)
    at_me = expert_id == me
    my_member = jnp.sum(jnp.where(at_me, member, 0.0), axis=1, keepdims=True)
    my_rank = jnp.sum(jnp.where(at_me, rank, 0.0), axis=1, keepdims=True)
    my_share = jnp.sum(jnp.where(at_me, share_table, 0.0), axis=1, keepdims=True)
    slot_col = lax.broadcasted_iota(jnp.int32, (n_tok, slots), 1)
    token_row = lax.broadcasted_iota(jnp.int32, (n_tok, slots), 0)
    fits = (
        (my_member > 0.5)
        & (my_rank == lax.rem(slot_col, half_slots).astype(f32))
        & (token_row // part_rows == slot_col // half_slots)
    )
    coef_row = jnp.sum(jnp.where(fits, my_share * scale_out, 0.0), axis=0, keepdims=True)
    diagonal = lax.broadcasted_iota(jnp.int32, (slots, slots), 0) == lax.broadcasted_iota(
        jnp.int32, (slots, slots), 1
    )
    coef = jnp.sum(jnp.where(diagonal, coef_row, 0.0), axis=1, keepdims=True)

    for step in range(1, n_attn):
        src = lax.rem(a + step, n_attn)
        remote(
            value_in.at[src], value_in.at[src], value_sem.at[0, src], value_sem.at[1, src], (src, e, r)
        ).wait_recv()
    gathered = [value_in[i].astype(f32) for i in range(n_attn)]
    low = jnp.concatenate([v[:tokens] for v in gathered], axis=0).astype(bf16)
    high = jnp.concatenate([v[tokens:] for v in gathered], axis=0).astype(bf16)
    copies[1].wait()
    copies[2].wait()
    chunk = width_out // 2
    per_chunk = n_expert // 2
    for c in range(2):
        partial = dot_f32(low, wo[:rows_o, c * chunk : (c + 1) * chunk]) + dot_f32(
            high, wo[rows_o:, c * chunk : (c + 1) * chunk]
        )
        for k in range(per_chunk):
            left = partial[:, 2 * k * piece : (2 * k + 1) * piece]
            right = partial[:, (2 * k + 1) * piece : (2 * k + 2) * piece]
            for s in range(2):
                dest_e = c * per_chunk + k
                dest = dest_e * 2 + s
                lo, hi = s * part_rows, (s + 1) * part_rows
                part_out[dest] = jnp.concatenate([left[lo:hi], right[lo:hi]], axis=0).astype(bf16)

                @pl.when(dest != plane_me)
                def _():
                    remote(
                        part_out.at[dest],
                        part_in.at[plane_me],
                        part_sem.at[0, dest],
                        part_sem.at[1, plane_me],
                        (a, dest_e, s),
                    ).start()

    part_in[plane_me] = part_out[plane_me]
    for step in range(1, n_plane):
        src = lax.rem(plane_me + step, n_plane)
        target = (a, src // 2, lax.rem(src, 2))
        copy = remote(
            part_out.at[src], part_in.at[src], part_sem.at[0, src], part_sem.at[1, src], target
        )
        copy.wait_recv()
        sends.append(copy)
    projected = part_in[0].astype(f32)
    for k in range(1, n_plane):
        projected = projected + part_in[k].astype(f32)
    hidden = (res_piece + projected).astype(bf16)

    packed = dot_f32(comb_t, hidden).astype(bf16)
    for j in range(n_all):
        row_out[j] = packed[j * slots : (j + 1) * slots]
    for step in range(1, n_all):
        dest = lax.rem(me + step, n_all)
        target = (dest // n_expert, lax.rem(dest, n_expert), r)
        copy = remote(
            row_out.at[dest], row_in.at[r, me], row_sem.at[0, dest], row_sem.at[1, me], target
        )
        copy.start()
        sends.append(copy)
    row_in[r, me] = row_out[me]
    for step in range(1, n_all):
        src = lax.rem(me + step, n_all)
        target = (src // n_expert, lax.rem(src, n_expert), r)
        remote(
            row_out.at[src], row_in.at[r, src], row_sem.at[0, src], row_sem.at[1, src], target
        ).wait_recv()
    pair_rows = remote(
        row_in.at[r], row_in.at[r], pair_row_sem.at[0], pair_row_sem.at[1], (a, e, other)
    )
    pair_rows.start()
    sends.append(pair_rows)
    remote(
        row_in.at[other], row_in.at[other], pair_row_sem.at[0], pair_row_sem.at[1], (a, e, other)
    ).wait_recv()

    def expert_rows(k):
        first = row_in[0, k].astype(f32)
        second = row_in[1, k].astype(f32)
        return (
            jnp.concatenate([first[:half_slots], second[:half_slots]], axis=0),
            jnp.concatenate([first[half_slots:], second[half_slots:]], axis=0),
        )

    squares = jnp.zeros((slots, piece), f32)
    for k in range(n_all):
        left, right = expert_rows(k)
        squares = squares + left * left + right * right
    mean = jnp.sum(squares, axis=1, keepdims=True) / float(2 * n_all * piece)
    inverse = lax.rsqrt(mean + 1e-06)
    for k in range(n_all):
        left, right = expert_rows(k)
        normed[2 * k] = (left * inverse * gain_ref[2 * k]).astype(bf16)
        normed[2 * k + 1] = (right * inverse * gain_ref[2 * k + 1]).astype(bf16)

    for i in range(8):
        copies[3 + i].wait()

    def gate_step(k, carry):
        gate_sum, up_sum = carry
        rows = normed[k]
        span = pl.ds(pl.multiple_of(k * piece, 16), piece)
        return (gate_sum + dot_f32(rows, gate[span, :]), up_sum + dot_f32(rows, up[span, :]))

    zeros = jnp.zeros((slots, half_units), f32)
    gate_sum, up_sum = lax.fori_loop(0, 2 * n_all, gate_step, (zeros, zeros))
    activated = (gate_sum / (1.0 + jnp.exp(-gate_sum)) * up_sum).astype(bf16)
    for i in range(4):
        copies[11 + i].wait()

    n_chunk = n_all // 2
    span_d = 4 * piece

    def down_chunk(i):
        return lax.rem(me // 2 + 1 + i, n_chunk)

    def pair_copy(c):
        return remote(
            pair_out.at[c], pair_in.at[c], pair_sem.at[0, c], pair_sem.at[1, c], (a, e, other)
        )

    def back_copy(dest):
        target = (dest // n_expert, lax.rem(dest, n_expert), r)
        return remote(
            back_out.at[dest], back_in.at[me], back_sem.at[0, dest], back_sem.at[1, me], target
        )

    def send_back(c):
        pair_copy(c).wait_recv()
        both = pair_own[c] + pair_in[c]
        for p in range(2):
            dest = 2 * c + p
            left = both[:, 2 * p * piece : (2 * p + 1) * piece]
            right = both[:, (2 * p + 1) * piece : (2 * p + 2) * piece]
            back_out[dest] = jnp.concatenate([left, right], axis=0).astype(bf16)

            @pl.when(dest != me)
            def _():
                back_copy(dest).start()

    for i in range(n_chunk):
        c = down_chunk(i)
        result = dot_f32(activated, down[:, pl.ds(pl.multiple_of(c * span_d, 128), span_d)]) * coef
        upper, lower = result[:half_slots], result[half_slots:]
        pair_own[c] = jnp.where(r == 0, upper, lower)
        pair_out[c] = jnp.where(r == 0, lower, upper)
        pair_copy(c).start()
        if i > 0:
            send_back(down_chunk(i - 1))
    send_back(down_chunk(n_chunk - 1))
    back_in[me] = back_out[me]
    for step in range(1, n_all):
        src = lax.rem(me + step, n_all)
        target = (src // n_expert, lax.rem(src, n_expert), r)
        copy = remote(
            back_out.at[src], back_in.at[src], back_sem.at[0, src], back_sem.at[1, src], target
        )
        copy.wait_recv()
        sends.append(copy)
    returned = back_in[...].reshape(-1, piece)
    routed = dot_f32(comb, returned)
    out_ref[...] = (hidden.astype(f32) + routed).astype(bf16)
    for i in range(n_chunk):
        pair_copy(i).wait_send()
    for copy in sends:
        copy.wait_send()


def fused_device(
    queries,
    new_latent,
    cache_pool,
    local_len,
    spill_cache,
    spill_owner,
    w_uv,
    w_o,
    residual,
    norm_gain,
    route_ids,
    route_scores,
    w_gate,
    w_up,
    w_down,
):
    n_attn = lax.axis_size("attn")
    n_expert = lax.axis_size("expert")
    n_rep = lax.axis_size("rep")
    n_all = n_attn * n_expert
    width = new_latent.shape[1]
    piece = w_down.shape[1] // (2 * n_all)
    half_units = w_gate.shape[1] // n_rep
    rows_part = route_ids.shape[0] // n_rep
    slots = 8

    block = spill_cache.shape[1]
    gain = norm_gain.reshape(2 * n_all, 1, piece)

    vmem = pl.BlockSpec(memory_space=pltpu.VMEM)
    smem = pl.BlockSpec(memory_space=pltpu.SMEM)
    hbm = pl.BlockSpec(memory_space=pl.ANY)
    bf16 = jnp.bfloat16
    n_plane = n_expert * n_rep
    dma = pltpu.SemaphoreType.DMA
    tokens = queries.shape[0]
    value_width = w_uv.shape[0] * w_uv.shape[2] // 2
    out = pl.pallas_call(
        layer_kernel,
        out_shape=jax.ShapeDtypeStruct((2 * rows_part, piece), bf16),
        in_specs=[vmem] * 4 + [smem] * 2 + [vmem] * 4 + [hbm] * 5,
        out_specs=vmem,
        scratch_shapes=[
            pltpu.VMEM(w_uv.shape, bf16),
            pltpu.VMEM(w_o.shape, bf16),
            pltpu.VMEM((w_gate.shape[0], half_units), bf16),
            pltpu.VMEM((w_up.shape[0], half_units), bf16),
            pltpu.VMEM((half_units, w_down.shape[1]), bf16),
            pltpu.VMEM((n_attn, CAP, block, width), bf16),
            pltpu.VMEM((n_attn, CAP, block, width), bf16),
            pltpu.VMEM((n_attn, 2 * tokens, value_width), bf16),
            pltpu.VMEM((n_plane, 2 * rows_part, piece), bf16),
            pltpu.VMEM((n_plane, 2 * rows_part, piece), bf16),
            pltpu.VMEM((n_all, 2 * slots, piece), bf16),
            pltpu.VMEM((n_rep, n_all, 2 * slots, piece), bf16),
            pltpu.VMEM((2 * n_all, 2 * slots, piece), bf16),
            pltpu.VMEM((n_all // 2, slots, 4 * piece), jnp.float32),
            pltpu.VMEM((n_all // 2, slots, 4 * piece), jnp.float32),
            pltpu.VMEM((n_all // 2, slots, 4 * piece), jnp.float32),
            pltpu.VMEM((n_all, 2 * slots, piece), bf16),
            pltpu.VMEM((n_all, 2 * slots, piece), bf16),
            dma((15,)),
            dma((2, n_attn)),
            dma((2, n_attn)),
            dma((2, n_plane)),
            dma((2, n_all)),
            dma((2,)),
            dma((2, n_all // 2)),
            dma((2, n_all)),
        ],
        compiler_params=pltpu.CompilerParams(
            collective_id=0, has_side_effects=True, vmem_limit_bytes=60 * 1024 * 1024
        ),
    )(
        queries,
        new_latent,
        cache_pool,
        spill_cache,
        local_len,
        spill_owner,
        residual,
        gain,
        route_ids,
        route_scores,
        w_uv,
        w_o,
        w_gate,
        w_up,
        w_down,
    )
    return jnp.concatenate([out[:rows_part], out[rows_part:]], axis=1)


def solution(mesh):
    n_attn, n_expert, n_rep = (mesh.shape[name] for name in ("attn", "expert", "rep"))
    fused = n_attn * n_expert == EXPERTS and n_attn == 4 and n_rep == 2
    return jax.shard_map(
        fused_device if fused else per_device,
        mesh=mesh,
        in_specs=(
            P("attn", ("expert", "rep")),
            P("attn", None),
            P("attn", None),
            P("attn", None),
            P("attn", None, None),
            P(),
            P(("expert", "rep"), None, None),
            P(("expert", "rep"), "attn"),
            P(None, "attn"),
            P(),
            P(),
            P(),
            P(None, ("attn", "expert")),
            P(None, ("attn", "expert")),
            P(("attn", "expert"), None),
        ),
        out_specs=P("rep", ("attn", "expert")),
        check_vma=False,
    )
```
